32 devices in a mesh: lat: 16 (over z, x, core), lon: 2 (over y).
Axes of the slice: x: 2, y: 2, z: 4, core: 2. Of those that a mesh axis runs over, the one named last changes fastest.
Arguments:
- tokens: bfloat16 [4, 96, 24, 512], P(None, 'lat', 'lon'), may hold values from -6 to 6
- w_qkv: bfloat16 [512, 1536], P('lon'), may hold values from -0.25 to 0.25
- w_out: bfloat16 [512, 512], P('lon'), may hold values from -0.25 to 0.25
- gain: float32 [512], replicated, may hold values from 0.1 to 1.9
- tau: float32 [8], replicated, may hold values from 1 to 12
- cotangent: bfloat16 [4, 96, 24, 512], P(None, 'lat', 'lon'), may hold values from -6 to 6
Outputs:
- output: bfloat16 [4, 96, 24, 512], P(None, 'lat', 'lon')
- grad_tokens: bfloat16 [4, 96, 24, 512], P(None, 'lat', 'lon')
- grad_qkv: float32 [512, 1536], P('lon')
- grad_out: float32 [512, 512], P('lon')
The draws below stay inside these ranges and needn't reach their ends.
All inputs are finite; a program needn't handle non-finite values.
Results may differ from the reference program's by a relative error of at most 0.035.
Values may be sent and summed in bfloat16 or wider, within the bound.
A program may use at most 128 MiB of HBM per device.

```python
import math
import jax
import jax.numpy as jnp
from jax import lax

D = 512
HEADS = 8
LV = 4
WL = 2
WH = 6
WW = 12
HD = 64
KEYS = 288
NH = 96
NW = 24


def with_spikes(values, rng, source, target, blocks, factor):
    owner, partner = [(jnp.arange(values.shape[dim]) // (values.shape[dim] // blocks)).reshape([-1 if axis == dim else 1 for axis in range(values.ndim)]) for dim in (source, target)]
    chosen = jax.random.permutation(rng, blocks)[partner]
    strong = (owner == chosen) | (owner == (partner + blocks // 2) % blocks)
    return jnp.where(strong, factor * values, values)


def shard_levels(own_key, shape, cuts, least, largest):
    factor_of, own = 1.0, jax.random.fold_in(own_key, 6)
    for dim, shards_of in cuts:
        steps = jnp.exp(jax.random.uniform(jax.random.fold_in(own, dim), (shards_of,), jnp.float32, least / len(cuts), largest / len(cuts)))
        factor_of = factor_of * jnp.repeat(steps, shape[dim] // shards_of).reshape([-1 if axis == dim else 1 for axis in range(len(shape))])
    return factor_of


def centred(own_key, shape, scale, bound, shards=(), held_as=jnp.bfloat16):
    array = jax.random.normal(own_key, shape, jnp.float32) * scale
    if len(shards) > 0:
        array = shard_levels(own_key, shape, shards, -0.22, 0.18) * array
    return jnp.clip(array, min=-bound, max=bound).astype(held_as)


def gaussian_with(key, shape, scale, most, pieces, heavy, dtype=jnp.bfloat16):
    result = scale * jax.random.normal(key, shape, jnp.float32)
    if pieces:
        result = result * shard_levels(key, shape, pieces, -0.22, 0.18)
    return jnp.clip(with_spikes(result, jax.random.fold_in(key, 3), *heavy), -most, most).astype(dtype)


def setup_inputs(seed: int = 0) -> dict:
    key_of = jax.random.split(jax.random.key(seed), 7)
    tokens = gaussian_with(key_of[0], (LV, NH, NW, D), 1.0, 6.0, ((1, 16), (2, 2)), (2, 3, 2, 2.0))
    w_qkv = centred(key_of[1], (D, 3 * D), D ** -0.5, 0.25, ((0, 2),))
    w_out = centred(key_of[2], (D, D), D ** -0.5, 0.25, ((0, 2),))
    gain = jnp.clip(1.0 + 0.18 * jax.random.normal(key_of[3], (D,), jnp.float32), 0.1, 1.9)
    tau = jnp.clip(jnp.exp(jax.random.uniform(key_of[4], (HEADS,), jnp.float32, math.log(1.0), math.log(12.0))), 1.0, 12.0)
    cotangent = centred(key_of[5], (LV, NH, NW, D), 1.0, 6.0, ((1, 16), (2, 2)))
    return dict(tokens=tokens, w_qkv=w_qkv, w_out=w_out, gain=gain, tau=tau, cotangent=cotangent)


NORM_EPS = 1e-05
UNIT_EPS = 1e-06

def unit_rows(vectors):
    scaling = lax.rsqrt(lax.optimization_barrier(jnp.sum(vectors * vectors, axis=-1, keepdims=True)) + UNIT_EPS)
    return (vectors * scaling, scaling)

def unit_back(vectors, scaling, gradient):
    inner_sum = lax.optimization_barrier(jnp.sum(vectors * gradient, axis=-1, keepdims=True))
    return scaling * (gradient - vectors * (inner_sum * scaling * scaling))

def norm_forward(y_rows):
    centered = y_rows - lax.optimization_barrier(jnp.mean(y_rows, axis=-1, keepdims=True))
    inverse = lax.rsqrt(lax.optimization_barrier(jnp.mean(centered * centered, axis=-1, keepdims=True)) + NORM_EPS)
    return (centered * inverse, inverse)

def norm_back(normed, inverse, upstream):
    mean_up = lax.optimization_barrier(jnp.mean(upstream, axis=-1, keepdims=True))
    mean_cross = lax.optimization_barrier(jnp.mean(upstream * normed, axis=-1, keepdims=True))
    return inverse * (upstream - mean_up - normed * mean_cross)

def to_windows(field):
    channels = field.shape[-1]
    rolled = jnp.roll(field, WW // 2, axis=2)
    padded = jnp.pad(rolled, ((0, 0), (WH // 2, WH // 2), (0, 0), (0, 0)))
    shaped = padded.reshape(LV, (NH + WH) // WH, WH, NW // WW, WW, channels)
    return shaped.transpose(1, 3, 0, 2, 4, 5).reshape((NH + WH) // WH, NW // WW, KEYS, channels)

def from_windows(windows):
    channels = windows.shape[-1]
    shaped = windows.reshape((NH + WH) // WH, NW // WW, LV, WH, WW, channels)
    padded = shaped.transpose(2, 0, 3, 1, 4, 5).reshape(LV, NH + WH, NW, channels)
    return jnp.roll(padded[:, WH // 2:WH // 2 + NH], -(WW // 2), axis=2)

def window_masks():
    token_ids = jnp.arange(KEYS)
    level_win = (token_ids // (WH * WW) + WL // 2) // WL
    same_level = level_win[:, None] == level_win[None, :]
    win_ids = jnp.arange((NH + WH) // WH)
    padded_row = WH * win_ids[:, None] + token_ids[None, :] // WW % WH
    inside = (padded_row >= WH // 2) & (padded_row < WH // 2 + NH)
    return (same_level[None, :, :] & inside[:, None, :]).astype(jnp.float32)

def reference(tokens, w_qkv, w_out, gain, tau, cotangent):
    flat_tok = tokens.reshape(-1, D)
    projected = jnp.dot(flat_tok, w_qkv, preferred_element_type=jnp.float32).astype(jnp.bfloat16)
    query_f = projected[:, :D].astype(jnp.float32).reshape(-1, HEADS, HD)
    key_f = projected[:, D:2 * D].astype(jnp.float32).reshape(-1, HEADS, HD)
    query_n, query_scale = unit_rows(query_f)
    key_n, key_scale = unit_rows(key_f)
    query_b = query_n.astype(jnp.bfloat16).reshape(LV, NH, NW, D)
    key_b = key_n.astype(jnp.bfloat16).reshape(LV, NH, NW, D)
    value_b = projected[:, 2 * D:].reshape(LV, NH, NW, D)
    win_shape = ((NH + WH) // WH, NW // WW, KEYS, HEADS, HD)
    query_w = to_windows(query_b).reshape(win_shape)
    key_w = to_windows(key_b).reshape(win_shape)
    value_w = to_windows(value_b).reshape(win_shape)
    masks = window_masks()
    temper = tau[:, None, None]

    def attention_probs(q_win, k_win, mask_win):
        scores = jnp.einsum('wqhd,wkhd->whqk', q_win.astype(jnp.float32), k_win.astype(jnp.float32)) * temper
        weights = jnp.exp(scores) * mask_win[None, None]
        return weights / lax.optimization_barrier(jnp.sum(weights, axis=-1, keepdims=True))

    def forward_win(operands):
        q_win, k_win, v_win, mask_win = operands
        probs = attention_probs(q_win, k_win, mask_win)
        probs_b = lax.optimization_barrier(probs.astype(jnp.bfloat16)).astype(jnp.float32)
        mixed = jnp.einsum('whqk,wkhd->wqhd', probs_b, v_win.astype(jnp.float32))
        return mixed.astype(jnp.bfloat16)
    attended_w = lax.map(forward_win, (query_w, key_w, value_w, masks))
    attended = from_windows(attended_w.reshape(win_shape[:3] + (D,))).reshape(-1, D)
    y_rows = jnp.dot(attended, w_out, preferred_element_type=jnp.float32)
    normed, inverse = norm_forward(y_rows)
    output = (flat_tok.astype(jnp.float32) + gain * normed).astype(jnp.bfloat16)
    upstream = gain * cotangent.reshape(-1, D).astype(jnp.float32)
    grad_y = norm_back(normed, inverse, upstream).astype(jnp.bfloat16)
    grad_out = jnp.dot(attended.T, grad_y, preferred_element_type=jnp.float32)
    grad_att = jnp.dot(grad_y, w_out.T, preferred_element_type=jnp.float32).astype(jnp.bfloat16)
    grad_att_w = to_windows(grad_att.reshape(LV, NH, NW, D)).reshape(win_shape)

    def backward_win(operands):
        q_win, k_win, v_win, d_win, mask_win = operands
        probs = attention_probs(q_win, k_win, mask_win)
        probs_b = lax.optimization_barrier(probs.astype(jnp.bfloat16)).astype(jnp.float32)
        grad_f = d_win.astype(jnp.float32)
        dprob = jnp.einsum('wqhd,wkhd->whqk', grad_f, v_win.astype(jnp.float32))
        total_sum = lax.optimization_barrier(jnp.sum(probs * dprob, axis=-1, keepdims=True))
        dscore = temper * (probs * (dprob - total_sum))
        dscore = lax.optimization_barrier(dscore.astype(jnp.bfloat16)).astype(jnp.float32)
        dquery = jnp.einsum('whqk,wkhd->wqhd', dscore, k_win.astype(jnp.float32))
        dkey = jnp.einsum('whqk,wqhd->wkhd', dscore, q_win.astype(jnp.float32))
        dvalue = jnp.einsum('whqk,wqhd->wkhd', probs_b, grad_f)
        return (dquery, dkey, dvalue)
    dquery_w, dkey_w, dvalue_w = lax.map(backward_win, (query_w, key_w, value_w, grad_att_w, masks))
    flat_shape = win_shape[:3] + (D,)
    dquery = from_windows(dquery_w.reshape(flat_shape)).reshape(-1, HEADS, HD)
    dkey = from_windows(dkey_w.reshape(flat_shape)).reshape(-1, HEADS, HD)
    dvalue = from_windows(dvalue_w.reshape(flat_shape)).reshape(-1, D)
    grad_q = unit_back(query_f, query_scale, dquery).reshape(-1, D)
    grad_k = unit_back(key_f, key_scale, dkey).reshape(-1, D)
    grad_proj = jnp.concatenate([grad_q, grad_k, dvalue], axis=1).astype(jnp.bfloat16)
    grad_qkv = jnp.dot(flat_tok.T, grad_proj, preferred_element_type=jnp.float32)
    grad_tok = cotangent.reshape(-1, D).astype(jnp.float32) + jnp.dot(grad_proj, w_qkv.T, preferred_element_type=jnp.float32)
    grad_tokens = grad_tok.astype(jnp.bfloat16).reshape(LV, NH, NW, D)
    return (output.reshape(LV, NH, NW, D), grad_tokens, grad_qkv, grad_out)
```

```python
import functools

import jax
import jax.numpy as jnp
from jax import lax
from jax.experimental import pallas as pl
from jax.experimental.pallas import tpu as pltpu
from jax.sharding import PartitionSpec as P

LV = 4
WH = 6
WW = 12
NORM_EPS = 1e-05
UNIT_EPS = 1e-06
MESH = pl.DeviceIdType.MESH
BF = jnp.bfloat16
F32 = jnp.float32
LEVELS = (0, 3, 1, 2)


def dot(a, b, ca, cb):
    return lax.dot_general(a, b, (((ca,), (cb,)), ((), ())), preferred_element_type=F32)


def bits_of(n):
    return n.bit_length() - 1


def norm_forward(y_rows):
    centered = y_rows - jnp.mean(y_rows, axis=-1, keepdims=True)
    inverse = lax.rsqrt(jnp.mean(centered * centered, axis=-1, keepdims=True) + NORM_EPS)
    return centered * inverse, inverse


def norm_back(normed, inverse, upstream):
    mean_up = jnp.mean(upstream, axis=-1, keepdims=True)
    mean_cross = jnp.mean(upstream * normed, axis=-1, keepdims=True)
    return inverse * (upstream - mean_up - normed * mean_cross)


class Copies:
    def __init__(self, send, recv):
        self.send, self.recv, self.used = send, recv, 0

    def make(self, src, dst, device):
        n = self.used
        self.used += 1
        return pltpu.make_async_remote_copy(
            src_ref=src, dst_ref=dst, send_sem=self.send.at[n], recv_sem=self.recv.at[n],
            device_id=device, device_id_type=MESH,
        )


def kernel(nlat, nlon, x_ref, wq_ref, wo_ref, gain_ref, tau_ref, home_ref, g_ref,
           xq, w, tok, proj, qn, kn, probs, att, dy, da, dqkv, oq, oq_in,
           f0, f1, r0, r1, a0, a1, send, recv):
    lat, lon = lax.axis_index("lat"), lax.axis_index("lon")
    D = 512
    R = D // nlon
    H = R // 2
    core = lat % 2
    sibling = lat + 1 - 2 * core

    def flip(index, bit):
        v = (index // (1 << bit)) % 2
        return index + (1 - 2 * v) * (1 << bit), v

    def ahead(a, b):
        return ((lat + a) % nlat, (lon + b) % nlon)

    def behind(a, b):
        return ((lat + nlat - a) % nlat, (lon + nlon - b) % nlon)

    moves = ((0, 1), (1, 0), (1, 1))
    peers = [ahead(a, b) for a, b in moves] + [behind(a, b) for a, b in moves]
    peers += [(lat, (lon + d) % nlon) for d in range(1, nlon)]
    peers += [(flip(lat, b)[0], lon) for b in range(bits_of(nlat))]
    barrier = pltpu.get_barrier_semaphore()
    for device in peers:
        pl.semaphore_signal(barrier, inc=1, device_id=device, device_id_type=MESH)
    pl.semaphore_wait(barrier, len(peers))

    copies = Copies(send, recv)
    waits = []

    def w_source(p):
        if p < 3:
            return wq_ref.at[pl.ds(core * H, H), pl.ds(p * D, D)]
        return wo_ref.at[pl.ds(core * H, H), :]

    halo = []
    for a, b in moves:
        c = copies.make(x_ref.at[2 * a + b], xq.at[2 * (1 - a) + 1 - b], ahead(a, b))
        c.start()
        halo.append(c)
    across, forward = [], []
    for p in range(4):
        across.append([])
        for d in range(1, nlon):
            c = copies.make(w_source(p), w.at[p, pl.ds(lon * R + core * H, H), :],
                            (lat, (lon + d) % nlon))
            c.start()
            across[p].append(c)
    for p in range(4):
        row = []
        for d in range(1, nlon):
            first = ((lon + nlon - d) % nlon) * R + core * H
            part = w.at[p, pl.ds(first, H), :]
            row.append(copies.make(part, part, (sibling, lon)))
        forward.append(row)

    xq[3] = x_ref[0]
    for p in range(3):
        w[p, pl.ds(lon * R, R), :] = wq_ref[:, p * D:(p + 1) * D]
    w[3, pl.ds(lon * R, R), :] = wo_ref[...]

    for c in halo:
        c.wait_recv()
    to = lax.broadcasted_iota(jnp.int32, (288, 576), 0)
    src = lax.broadcasted_iota(jnp.int32, (288, 576), 1)
    want = ((to % 144) // 36) * 144 + (to // 144) * 36 + to % 36
    flat = xq[...].reshape(576, D)
    tokens = dot((want == src).astype(BF), flat, 1, 0).astype(BF)
    cot = dot((want + 72 == src).astype(BF), flat, 1, 0)
    tok[...] = tokens

    def arrive(p):
        for c in across[p]:
            c.wait_recv()
        for c in forward[p]:
            c.start()

    def project(p):
        for c in forward[p]:
            c.wait_recv()
        proj[p] = dot(tok[...], w[p], 1, 0).astype(BF)

    arrive(0)
    arrive(1)
    project(0)
    arrive(2)
    project(1)
    arrive(3)
    project(2)

    kk = lax.broadcasted_iota(jnp.int32, (144, 144), 0)
    qq = lax.broadcasted_iota(jnp.int32, (144, 144), 1)
    rows_ok = ((kk // 72) == (qq // 72)) | (jnp.zeros_like(kk) + lat != 0)
    level_ok = ((kk % 36) // 18) == ((qq % 36) // 18)

    def place(step):
        g, pair = step // 4, step % 4
        return (g, pair, pl.ds(pl.multiple_of(g * 144, 16), 144),
                pl.ds(pl.multiple_of(pair * 128, 128), 128))

    def halves(x):
        return x[:, :64], x[:, 64:]

    def unit(x):
        x = x.astype(F32)
        return (x * lax.rsqrt(jnp.sum(x * x, axis=-1, keepdims=True) + UNIT_EPS)).astype(BF)

    def forward_step(step, carry):
        g, pair, rs, cs = place(step)
        qs = [unit(x) for x in halves(proj[0, rs, cs])]
        ks = [unit(x) for x in halves(proj[1, rs, cs])]
        qn[rs, cs] = jnp.concatenate(qs, axis=1)
        kn[rs, cs] = jnp.concatenate(ks, axis=1)
        vs = halves(proj[2, rs, cs])
        mask = (rows_ok & (level_ok | (jnp.zeros_like(kk) + g == 1))).astype(F32)
        outs = []
        for i in range(2):
            s = dot(ks[i], qs[i], 1, 1) * tau_ref[2 * pair + i]
            e = jnp.exp(s) * mask
            p = e * (1.0 / jnp.sum(e, axis=0, keepdims=True))
            probs[2 * step + i] = p
            outs.append(dot(p.astype(BF), vs[i], 0, 0))
        att[rs, cs] = jnp.concatenate(outs, axis=1).astype(BF)
        return carry

    lax.fori_loop(0, 8, forward_step, 0)

    for c in forward[3]:
        c.wait_recv()
    normed, inverse = norm_forward(dot(att[...], w[3], 1, 0))
    gain = gain_ref[...]
    output = (tok[...].astype(F32) + gain * normed).astype(BF)
    dy[...] = norm_back(normed, inverse, gain * cot).astype(BF)
    da[...] = dot(dy[...], w[3], 1, 1).astype(BF)

    def dv_step(step, carry):
        g, pair, rs, cs = place(step)
        das = halves(da[rs, cs])
        dqkv[2, rs, cs] = jnp.concatenate(
            [dot(probs[2 * step + i].astype(BF), das[i], 1, 0) for i in range(2)], axis=1
        ).astype(BF)
        return carry

    lax.fori_loop(0, 8, dv_step, 0)

    half = 4 * D

    def place_gradient(f, which, grad, lon_first):
        for b in range(nlon):
            for ch in range(4):
                if lon_first:
                    first = which * half + b * 4 * R + ch * R
                else:
                    first = which * half + (ch // 2) * (half // 2) + b * 2 * R + (ch % 2) * R
                f[first:first + R, :] = grad[b * R:(b + 1) * R, ch * 128:(ch + 1) * 128]

    lat_bits = [("lat", b) for b in range(bits_of(nlat))]
    lon_bits = [("lon", b) for b in reversed(range(bits_of(nlon)))]

    class Stream:
        def __init__(self, f, r, a, order):
            self.f, self.r, self.a, self.order = f, r, a, order
            self.stage, self.size, self.off = 0, 2 * half, 0
            self.gsize, self.goff = 2 * half // nlon, 0
            self.done, self.gathers = [], []

        def start(self):
            axis, bit = self.order[self.stage]
            self.size //= 2
            peer, mine = flip(lat if axis == "lat" else lon, bit)
            device = (peer, lon) if axis == "lat" else (lat, peer)
            self.base = 4 * half - 4 * self.size if False else 2 * half - 2 * self.size
            give = pl.multiple_of(self.off + (1 - mine) * self.size, 16)
            self.off = self.off + mine * self.size
            if axis == "lat":
                self.gsize //= 2
                self.gathers.append((device, self.gsize))
                self.goff = self.goff + mine * self.gsize
                self.gathers[-1] = (device, self.gsize, self.goff)
            self.copy = copies.make(self.f.at[pl.ds(give, self.size), :],
                                    self.r.at[pl.ds(self.base, self.size), :], device)
            self.copy.start()

        def finish(self):
            self.copy.wait_recv()
            self.done.append(self.copy)
            keep = pl.ds(pl.multiple_of(self.off, 16), self.size)
            total = (self.f[keep, :].astype(F32)
                     + self.r[self.base:self.base + self.size, :].astype(F32)).astype(BF)
            self.stage += 1
            if self.stage == len(self.order):
                self.a[pl.ds(pl.multiple_of(self.goff, 16), self.size), :] = total
            else:
                self.f[keep, :] = total

        def gather_start(self):
            device, size, off = self.gathers.pop()
            part = self.a.at[pl.ds(pl.multiple_of(off, 16), size), :]
            self.copy = copies.make(part, part, device)
            self.copy.start()

        def gather_finish(self):
            self.copy.wait_recv()
            self.done.append(self.copy)

    s0 = Stream(f0, r0, a0, lat_bits[:1] + lon_bits + lat_bits[1:])
    s1 = Stream(f1, r1, a1, lat_bits[:2] + lon_bits + lat_bits[2:])

    place_gradient(f0, 0, dot(att[...], dy[...], 0, 0).astype(BF), True)
    place_gradient(f0, 1, dot(tok[...], dqkv[2], 0, 0).astype(BF), True)
    s0.start()

    def back(x, n, grad):
        x = x.astype(F32)
        scale = lax.rsqrt(jnp.sum(x * x, axis=-1, keepdims=True) + UNIT_EPS)
        inner = jnp.sum(x * grad, axis=-1, keepdims=True)
        return scale * (grad - x * (inner * scale * scale))

    def ds_step(step, carry):
        g, pair, rs, cs = place(step)
        das, vs = halves(da[rs, cs]), halves(proj[2, rs, cs])
        qs, ks = halves(proj[0, rs, cs]), halves(proj[1, rs, cs])
        qns, kns = halves(qn[rs, cs]), halves(kn[rs, cs])
        dqs, dks = [], []
        for i in range(2):
            p = probs[2 * step + i]
            dp = dot(vs[i], das[i], 1, 1)
            tot = jnp.sum(p * dp, axis=0, keepdims=True)
            ds = (tau_ref[2 * pair + i] * (p * (dp - tot))).astype(BF)
            dqs.append(back(qs[i], qns[i], dot(ds, kns[i], 0, 0)))
            dks.append(back(ks[i], kns[i], dot(ds, qns[i], 1, 0)))
        dqkv[0, rs, cs] = jnp.concatenate(dqs, axis=1).astype(BF)
        dqkv[1, rs, cs] = jnp.concatenate(dks, axis=1).astype(BF)
        return carry

    lax.fori_loop(0, 8, ds_step, 0)

    s0.finish()
    s0.start()
    place_gradient(f1, 0, dot(tok[...], dqkv[0], 0, 0).astype(BF), False)
    place_gradient(f1, 1, dot(tok[...], dqkv[1], 0, 0).astype(BF), False)
    s1.start()

    grad_in = dot(dqkv[0], w[0], 1, 1) + dot(dqkv[1], w[1], 1, 1) + dot(dqkv[2], w[2], 1, 1)
    grad_tok = (cot + grad_in).astype(BF)
    to2 = lax.broadcasted_iota(jnp.int32, (576, 288), 0)
    src2 = lax.broadcasted_iota(jnp.int32, (576, 288), 1)
    inner = to2 % 144
    want2 = ((inner % 72) // 36) * 144 + (to2 // 144) * 36 + inner % 36
    first = ((want2 == src2) & (inner < 72)).astype(BF)
    second = ((want2 == src2) & (inner >= 72)).astype(BF)
    oq[...] = (dot(first, output, 1, 0) + dot(second, grad_tok, 1, 0)).astype(BF).reshape(4, 144, D)
    s1.finish()
    s1.start()
    homes = []
    for a, b in moves:
        c = copies.make(oq.at[2 * (1 - a) + 1 - b], oq_in.at[2 * a + b - 1], behind(a, b))
        c.start()
        homes.append(c)
    home_ref[0] = oq[3]

    total = len(s0.order)
    while s1.stage < total:
        if s0.stage < total:
            s0.finish()
            if s0.stage < total:
                s0.start()
            else:
                s0.gather_start()
        s1.finish()
        if s1.stage < total:
            s1.start()
    s1.gather_start()
    while True:
        s0.gather_finish()
        if s0.gathers:
            s0.gather_start()
        s1.gather_finish()
        if not s1.gathers:
            break
        s1.gather_start()
    if len(s0.gathers) > 0:
        raise ValueError

    for which, (a, p) in enumerate(((a0, 3), (a0, 2), (a1, 0), (a1, 1))):
        for ch in range(4):
            first = (which % 2) * (half // nlon) + ch * R
            g_ref[:, p * D + ch * 128:p * D + (ch + 1) * 128] = a[first:first + R, :]
    for i, c in enumerate(homes):
        c.wait_recv()
        home_ref[i + 1] = oq_in[i]
    for c in halo + homes + sum(across, []) + sum(forward, []) + s0.done + s1.done:
        c.wait_send()


def on_device(nlat, nlon, tokens, w_qkv, w_out, gain, tau, cotangent):
    D = tokens.shape[3]

    def quarters(x):
        x = jnp.stack([x[l] for l in LEVELS])
        x = x.reshape(LV, 2, WH // 2, 2, WW // 2, D).transpose(1, 3, 0, 2, 4, 5)
        return x.reshape(4, 72, D)

    x = jnp.concatenate([quarters(tokens), quarters(cotangent)], axis=1)
    R = D // nlon
    half = 4 * D
    n_copies = 6 + 8 * (nlon - 1) + 2 * (2 * bits_of(nlat) + bits_of(nlon))
    vm = pl.BlockSpec(memory_space=pltpu.VMEM)
    home, grads = pl.pallas_call(
        functools.partial(kernel, nlat, nlon),
        out_shape=(
            jax.ShapeDtypeStruct((4, 144, D), BF),
            jax.ShapeDtypeStruct((R, 4 * D), BF),
        ),
        in_specs=[vm] * 4 + [pl.BlockSpec(memory_space=pltpu.SMEM)],
        out_specs=(vm, vm),
        scratch_shapes=[
            pltpu.VMEM((4, 144, D), BF),
            pltpu.VMEM((4, D, D), BF),
            pltpu.VMEM((288, D), BF),
            pltpu.VMEM((3, 288, D), BF),
            pltpu.VMEM((288, D), BF),
            pltpu.VMEM((288, D), BF),
            pltpu.VMEM((16, 144, 144), F32),
            pltpu.VMEM((288, D), BF),
            pltpu.VMEM((288, D), BF),
            pltpu.VMEM((288, D), BF),
            pltpu.VMEM((3, 288, D), BF),
            pltpu.VMEM((4, 144, D), BF),
            pltpu.VMEM((3, 144, D), BF),
            pltpu.VMEM((2 * half, 128), BF),
            pltpu.VMEM((2 * half, 128), BF),
            pltpu.VMEM((2 * half, 128), BF),
            pltpu.VMEM((2 * half, 128), BF),
            pltpu.VMEM((2 * half // nlon, 128), BF),
            pltpu.VMEM((2 * half // nlon, 128), BF),
            pltpu.SemaphoreType.DMA((n_copies,)),
            pltpu.SemaphoreType.DMA((n_copies,)),
        ],
        compiler_params=pltpu.CompilerParams(
            collective_id=0, has_side_effects=True, vmem_limit_bytes=48 * 1024 * 1024
        ),
    )(x, w_qkv, w_out, gain.reshape(1, D), tau)

    def grid(q):
        q = q.reshape(2, 2, LV, WH // 2, WW // 2, D).transpose(2, 0, 3, 1, 4, 5)
        q = q.reshape(LV, WH, WW, D)
        return jnp.stack([q[LEVELS.index(l)] for l in range(LV)])

    return (
        grid(home[:, :72]),
        grid(home[:, 72:]),
        grads[:, : 3 * D].astype(F32),
        grads[:, 3 * D :].astype(F32),
    )


def solution(mesh):
    nlat, nlon = mesh.shape["lat"], mesh.shape["lon"]
    grid = P(None, "lat", "lon", None)
    rows = P("lon", None)
    return jax.shard_map(
        functools.partial(on_device, nlat, nlon),
        mesh=mesh,
        in_specs=(grid, rows, rows, P(), P(), grid),
        out_specs=(grid, grid, rows, rows),
        check_vma=False,
    )
```

```python
import functools

import jax
import jax.numpy as jnp
import numpy as np
from jax import lax
from jax.experimental import pallas as pl
from jax.experimental.pallas import tpu as pltpu
from jax.sharding import PartitionSpec as P

LV = 4
WH = 6
WW = 12
NORM_EPS = 1e-05
UNIT_EPS = 1e-06
MESH = pl.DeviceIdType.MESH
BF = jnp.bfloat16
F32 = jnp.float32
LEVELS = (0, 3, 1, 2)


def dot(a, b, ca, cb):
    return lax.dot_general(a, b, (((ca,), (cb,)), ((), ())), preferred_element_type=F32)


def bits_of(n):
    return n.bit_length() - 1


def norm_forward(y_rows):
    centered = y_rows - jnp.mean(y_rows, axis=-1, keepdims=True)
    inverse = lax.rsqrt(jnp.mean(centered * centered, axis=-1, keepdims=True) + NORM_EPS)
    return centered * inverse, inverse


def norm_back(normed, inverse, upstream):
    mean_up = jnp.mean(upstream, axis=-1, keepdims=True)
    mean_cross = jnp.mean(upstream * normed, axis=-1, keepdims=True)
    return inverse * (upstream - mean_up - normed * mean_cross)


class Copies:
    def __init__(self, send, recv):
        self.send, self.recv, self.used = send, recv, 0

    def make(self, src, dst, device):
        n = self.used
        self.used += 1
        return pltpu.make_async_remote_copy(
            src_ref=src, dst_ref=dst, send_sem=self.send.at[n], recv_sem=self.recv.at[n],
            device_id=device, device_id_type=MESH,
        )


def kernel(nlat, nlon, t_ref, c_ref, wq_ref, wo_ref, gain_ref, split_ref, window_ref, tau_ref,
           out_ref, gt_ref, g_ref,
           xs, xo, xq, w, tok, proj, qn, kn, probs, att, dy, da, dqkv, oq, oh,
           f0, f1, r0, r1, a0, a1, send, recv):
    lat, lon = lax.axis_index("lat"), lax.axis_index("lon")
    D = 512
    R = D // nlon
    H = R // 2
    H4 = R // 4
    xbit = (lat // 2) % 2
    core = lat % 2
    sibling = lat + 1 - 2 * core

    def flip(index, bit):
        v = (index // (1 << bit)) % 2
        return index + (1 - 2 * v) * (1 << bit), v

    def ahead(a, b):
        return ((lat + a) % nlat, (lon + b) % nlon)

    def behind(a, b):
        return ((lat + nlat - a) % nlat, (lon + nlon - b) % nlon)

    moves = ((0, 1), (1, 0), (1, 1))
    peers = [ahead(a, b) for a, b in moves] + [behind(a, b) for a, b in moves]
    core_group = [("lat", 0)]
    plane = [("lat", 1)] + [("lon", b) for b in reversed(range(bits_of(nlon)))]
    rest = [("lat", b) for b in range(2, bits_of(nlat))]
    strips = [("lat", 1)] + rest

    def member(group, k):
        at, place_mine, place_there = {"lat": lat, "lon": lon}, 0, 0
        for n, (axis, bit) in enumerate(group):
            there, mine = flip({"lat": lat, "lon": lon}[axis], bit)
            flipped = (k >> (len(group) - 1 - n)) & 1
            if flipped:
                at[axis] = at[axis] + (1 - 2 * mine) * (1 << bit)
            place_mine = 2 * place_mine + mine
            place_there = 2 * place_there + (1 - mine if flipped else mine)
        return (at["lat"], at["lon"]), place_mine, place_there

    for group in (core_group, plane, rest, strips):
        peers += [member(group, k)[0] for k in range(1, 1 << len(group))]
    barrier = pltpu.get_barrier_semaphore()
    for device in peers:
        pl.semaphore_signal(barrier, inc=1, device_id=device, device_id_type=MESH)
    pl.semaphore_wait(barrier, len(peers))

    copies = Copies(send, recv)
    waits = []

    mine4 = core * H + xbit * H4

    def w_source(p):
        if p < 3:
            return wq_ref.at[pl.ds(mine4, H4), pl.ds(p * D, D)]
        return wo_ref.at[pl.ds(mine4, H4), :]

    across, through, forward = [[], [], [], []], [], []

    def cross(p):
        for d in range(1, nlon):
            c = copies.make(w_source(p), w.at[p, pl.ds(lon * R + mine4, H4), :],
                            (lat, (lon + d) % nlon))
            c.start()
            across[p].append(c)

    for p in range(3):
        cross(p)

    xs[...] = jnp.zeros_like(xs)
    halo = []
    for kind, ref in enumerate((t_ref, c_ref)):
        for l in range(LV):
            for r in range(WH):
                first = (l * WH + r) * 16
                xs[kind, first:first + WW, :] = ref[l, r]
        xo[kind] = dot(split_ref[...], xs[kind], 1, 0).astype(BF).reshape(4, 80, D)
        halo.append([])
        for a, b in moves:
            c = copies.make(xo.at[kind, 2 * a + b], xq.at[kind, 2 * (1 - a) + 1 - b], ahead(a, b))
            c.start()
            halo[kind].append(c)
        xq[kind, 3] = xo[kind, 0]
    cross(3)

    for p in range(4):
        one, two = [], []
        for d in range(1, nlon):
            there = ((lon + nlon - d) % nlon) * R
            part = w.at[p, pl.ds(there + mine4, H4), :]
            one.append(copies.make(part, part, (flip(lat, 1)[0], lon)))
            part = w.at[p, pl.ds(there + core * H, H), :]
            two.append(copies.make(part, part, (sibling, lon)))
        through.append(one)
        forward.append(two)

    for p in range(3):
        w[p, pl.ds(lon * R, R), :] = wq_ref[:, p * D:(p + 1) * D]
    w[3, pl.ds(lon * R, R), :] = wo_ref[...]

    def windowed(kind):
        for c in halo[kind]:
            c.wait_recv()
        return dot(window_ref[...], xq[kind].reshape(320, D), 1, 0)

    def pass_on(before, after, p):
        for c in before[p]:
            c.wait_recv()
        for c in after[p]:
            c.start()

    def project(p):
        for c in forward[p]:
            c.wait_recv()
        proj[p] = dot(tok[...], w[p], 1, 0).astype(BF)

    for p in range(3):
        pass_on(across, through, p)
    tok[...] = windowed(0).astype(BF)
    for p in range(3):
        pass_on(through, forward, p)
        project(p)
    pass_on(across, through, 3)

    kk = lax.broadcasted_iota(jnp.int32, (144, 144), 0)
    qq = lax.broadcasted_iota(jnp.int32, (144, 144), 1)
    rows_ok = ((kk // 72) == (qq // 72)) | (jnp.zeros_like(kk) + lat != 0)
    level_ok = ((kk % 36) // 18) == ((qq % 36) // 18)

    def place(step):
        g, pair = step // 4, step % 4
        return (g, pair, pl.ds(pl.multiple_of(g * 144, 16), 144),
                pl.ds(pl.multiple_of(pair * 128, 128), 128))

    def halves(x):
        return x[:, :64], x[:, 64:]

    def unit(x):
        x = x.astype(F32)
        return (x * lax.rsqrt(jnp.sum(x * x, axis=-1, keepdims=True) + UNIT_EPS)).astype(BF)

    def forward_step(step, carry):
        g, pair, rs, cs = place(step)
        qs = [unit(x) for x in halves(proj[0, rs, cs])]
        ks = [unit(x) for x in halves(proj[1, rs, cs])]
        qn[rs, cs] = jnp.concatenate(qs, axis=1)
        kn[rs, cs] = jnp.concatenate(ks, axis=1)
        vs = halves(proj[2, rs, cs])
        mask = (rows_ok & (level_ok | (jnp.zeros_like(kk) + g == 1))).astype(F32)
        outs = []
        for i in range(2):
            s = dot(ks[i], qs[i], 1, 1) * tau_ref[2 * pair + i]
            e = jnp.exp(s) * mask
            p = e * (1.0 / jnp.sum(e, axis=0, keepdims=True))
            probs[2 * step + i] = p
            outs.append(dot(p.astype(BF), vs[i], 0, 0))
        att[rs, cs] = jnp.concatenate(outs, axis=1).astype(BF)
        return carry

    lax.fori_loop(0, 2, forward_step, 0)
    pass_on(through, forward, 3)
    lax.fori_loop(2, 8, forward_step, 0)
    cot = windowed(1)

    for c in forward[3]:
        c.wait_recv()
    normed, inverse = norm_forward(dot(att[...], w[3], 1, 0))
    gain = gain_ref[...]
    output = (tok[...].astype(F32) + gain * normed).astype(BF)
    homes = []

    def send_home(kind, value):
        oq[kind] = dot(window_ref[...], value, 0, 0).astype(BF).reshape(4, 80, D)
        for a, b in moves:
            c = copies.make(oq.at[kind, 2 * (1 - a) + 1 - b], oh.at[kind, 2 * a + b], behind(a, b))
            c.start()
            homes.append(c)
        oh[kind, 0] = oq[kind, 3]

    dy[...] = norm_back(normed, inverse, gain * cot).astype(BF)
    da[...] = dot(dy[...], w[3], 1, 1).astype(BF)

    def dv_step(step, carry):
        g, pair, rs, cs = place(step)
        das = halves(da[rs, cs])
        dqkv[2, rs, cs] = jnp.concatenate(
            [dot(probs[2 * step + i].astype(BF), das[i], 1, 0) for i in range(2)], axis=1
        ).astype(BF)
        return carry

    lax.fori_loop(0, 8, dv_step, 0)

    half = 4 * D

    def place_gradient(f, which, grad):
        for b in range(nlon):
            for ch in range(4):
                first = which * half + (ch // 2) * (half // 2) + b * 2 * R + (ch % 2) * R
                f[first:first + R, :] = grad[b * R:(b + 1) * R, ch * 128:(ch + 1) * 128]

    class Stream:
        def __init__(self, f, r, a):
            self.f, self.r, self.a = f, r, a
            self.size, self.off, self.base = 2 * half, 0, 0
            self.gsize, self.goff = 2 * half // nlon, 0
            self.done = []

        def start(self, group):
            n = 1 << len(group)
            self.size //= n
            self.now = []
            for k in range(1, n):
                device, _, there = member(group, k)
                give = pl.multiple_of(self.off + there * self.size, 16)
                c = copies.make(self.f.at[pl.ds(give, self.size), :],
                                self.r.at[pl.ds(self.base, self.size), :], device)
                c.start()
                self.now.append((c, self.base))
                self.base += self.size
            self.off = self.off + member(group, 0)[1] * self.size
            for axis, bit in group:
                if axis == "lat":
                    self.gsize //= 2
                    self.goff = self.goff + flip(lat, bit)[1] * self.gsize

        def finish(self, last=False):
            keep = pl.ds(pl.multiple_of(self.off, 16), self.size)
            total = self.f[keep, :].astype(F32)
            for c, base in self.now:
                c.wait_recv()
                total = total + self.r[base:base + self.size, :].astype(F32)
            self.done += [c for c, _ in self.now]
            if last:
                self.a[pl.ds(pl.multiple_of(self.goff, 16), self.size), :] = total.astype(BF)
            else:
                self.f[keep, :] = total.astype(BF)

        def gather(self, group, off, size):
            self.now = []
            part = self.a.at[pl.ds(pl.multiple_of(off, 16), size), :]
            for k in range(1, 1 << len(group)):
                c = copies.make(part, part, member(group, k)[0])
                c.start()
                self.now.append((c, 0))

        def gathered(self):
            for c, _ in self.now:
                c.wait_recv()
                self.done.append(c)

    s0 = Stream(f0, r0, a0)
    s1 = Stream(f1, r1, a1)
    half_rows = half // nlon

    place_gradient(f0, 0, dot(att[...], dy[...], 0, 0).astype(BF))
    place_gradient(f0, 1, dot(tok[...], dqkv[2], 0, 0).astype(BF))
    s0.start(core_group)
    send_home(0, output)

    def back(x, n, grad):
        x = x.astype(F32)
        scale = lax.rsqrt(jnp.sum(x * x, axis=-1, keepdims=True) + UNIT_EPS)
        inner = jnp.sum(x * grad, axis=-1, keepdims=True)
        return scale * (grad - x * (inner * scale * scale))

    def ds_step(step, carry):
        g, pair, rs, cs = place(step)
        das, vs = halves(da[rs, cs]), halves(proj[2, rs, cs])
        qs, ks = halves(proj[0, rs, cs]), halves(proj[1, rs, cs])
        qns, kns = halves(qn[rs, cs]), halves(kn[rs, cs])
        dqs, dks = [], []
        for i in range(2):
            p = probs[2 * step + i]
            dp = dot(vs[i], das[i], 1, 1)
            tot = jnp.sum(p * dp, axis=0, keepdims=True)
            ds = (tau_ref[2 * pair + i] * (p * (dp - tot))).astype(BF)
            dqs.append(back(qs[i], qns[i], dot(ds, kns[i], 0, 0)))
            dks.append(back(ks[i], kns[i], dot(ds, qns[i], 1, 0)))
        dqkv[0, rs, cs] = jnp.concatenate(dqs, axis=1).astype(BF)
        dqkv[1, rs, cs] = jnp.concatenate(dks, axis=1).astype(BF)
        return carry

    lax.fori_loop(0, 1, ds_step, 0)
    s0.finish()
    s0.start(plane)
    lax.fori_loop(1, 8, ds_step, 0)
    place_gradient(f1, 0, dot(tok[...], dqkv[0], 0, 0).astype(BF))
    place_gradient(f1, 1, dot(tok[...], dqkv[1], 0, 0).astype(BF))
    s1.start(core_group)
    s0.finish()
    s0.start(rest)
    s1.finish()
    s1.start(plane)

    grad_in = dot(dqkv[0], w[0], 1, 1) + dot(dqkv[1], w[1], 1, 1) + dot(dqkv[2], w[2], 1, 1)
    send_home(1, (cot + grad_in).astype(BF))
    s0.finish(True)
    s0.gather(strips, s0.goff, s0.gsize)
    s1.finish()
    s1.start(rest)
    s0.gathered()
    s0.gather(core_group, core * half_rows, half_rows)
    s1.finish(True)
    s1.gather(strips, s1.goff, s1.gsize)

    def bring(kind, ref):
        for c in homes[3 * kind:3 * kind + 3]:
            c.wait_recv()
        full = dot(split_ref[...], oh[kind].reshape(320, D), 0, 0).astype(BF)
        for l in range(LV):
            for r in range(WH):
                first = (l * WH + r) * 16
                ref[l, r] = full[first:first + WW, :]

    def collect(a, p, which):
        for ch in range(4):
            first = which * half_rows + ch * R
            g_ref[:, p * D + ch * 128:p * D + (ch + 1) * 128] = a[first:first + R, :]

    bring(0, out_ref)
    bring(1, gt_ref)
    s0.gathered()
    collect(a0, 3, 0)
    collect(a0, 2, 1)
    s1.gathered()
    s1.gather(core_group, core * half_rows, half_rows)
    s1.gathered()
    collect(a1, 0, 0)
    collect(a1, 1, 1)
    started = sum(halo + across + through + forward, []) + homes
    for c in started + s0.done + s1.done:
        c.wait_send()


def on_device(nlat, nlon, tokens, w_qkv, w_out, gain, tau, cotangent):
    D = tokens.shape[3]

    split = np.zeros((320, 384), np.float32)
    window = np.zeros((288, 320), np.float32)
    for q in range(4):
        for i in range(72):
            level, row, col = LEVELS[i // 18], 3 * (q // 2) + i % 18 // 6, 6 * (q % 2) + i % 6
            split[q * 80 + i, (level * WH + row) * 16 + col] = 1
            window[i // 36 * 144 + q * 36 + i % 36, q * 80 + i] = 1
    R = D // nlon
    half = 4 * D
    n_copies = 12 + 12 * (nlon - 1) + 2 * (2 * nlon - 1 + nlat // 4 - 1 + nlat // 2 - 1 + 2)
    vm = pl.BlockSpec(memory_space=pltpu.VMEM)
    output, grad_tokens, grads = pl.pallas_call(
        functools.partial(kernel, nlat, nlon),
        out_shape=(
            jax.ShapeDtypeStruct(tokens.shape, BF),
            jax.ShapeDtypeStruct(tokens.shape, BF),
            jax.ShapeDtypeStruct((R, 4 * D), BF),
        ),
        in_specs=[vm] * 7 + [pl.BlockSpec(memory_space=pltpu.SMEM)],
        out_specs=(vm, vm, vm),
        scratch_shapes=[
            pltpu.VMEM((2, 384, D), BF),
            pltpu.VMEM((2, 4, 80, D), BF),
            pltpu.VMEM((2, 4, 80, D), BF),
            pltpu.VMEM((4, D, D), BF),
            pltpu.VMEM((288, D), BF),
            pltpu.VMEM((3, 288, D), BF),
            pltpu.VMEM((288, D), BF),
            pltpu.VMEM((288, D), BF),
            pltpu.VMEM((16, 144, 144), F32),
            pltpu.VMEM((288, D), BF),
            pltpu.VMEM((288, D), BF),
            pltpu.VMEM((288, D), BF),
            pltpu.VMEM((3, 288, D), BF),
            pltpu.VMEM((2, 4, 80, D), BF),
            pltpu.VMEM((2, 4, 80, D), BF),
            pltpu.VMEM((2 * half, 128), BF),
            pltpu.VMEM((2 * half, 128), BF),
            pltpu.VMEM((2 * half, 128), BF),
            pltpu.VMEM((2 * half, 128), BF),
            pltpu.VMEM((2 * half // nlon, 128), BF),
            pltpu.VMEM((2 * half // nlon, 128), BF),
            pltpu.SemaphoreType.DMA((n_copies,)),
            pltpu.SemaphoreType.DMA((n_copies,)),
        ],
        compiler_params=pltpu.CompilerParams(
            collective_id=0, has_side_effects=True, vmem_limit_bytes=48 * 1024 * 1024
        ),
    )(tokens, cotangent, w_qkv, w_out, gain.reshape(1, D), jnp.asarray(split, BF),
      jnp.asarray(window, BF), tau)

    return (
        output,
        grad_tokens,
        grads[:, : 3 * D].astype(F32),
        grads[:, 3 * D :].astype(F32),
    )


def solution(mesh):
    nlat, nlon = mesh.shape["lat"], mesh.shape["lon"]
    grid = P(None, "lat", "lon", None)
    rows = P("lon", None)
    return jax.shard_map(
        functools.partial(on_device, nlat, nlon),
        mesh=mesh,
        in_specs=(grid, rows, rows, P(), P(), grid),
        out_specs=(grid, grid, rows, rows),
        check_vma=False,
    )
```

```python
import functools

import jax
import jax.numpy as jnp
import numpy as np
from jax import lax
from jax.experimental import pallas as pl
from jax.experimental.pallas import tpu as pltpu
from jax.sharding import PartitionSpec as P

LV = 4
WH = 6
WW = 12
NORM_EPS = 1e-05
UNIT_EPS = 1e-06
MESH = pl.DeviceIdType.MESH
BF = jnp.bfloat16
F32 = jnp.float32
LEVELS = (0, 3, 1, 2)


def dot(a, b, ca, cb):
    return lax.dot_general(a, b, (((ca,), (cb,)), ((), ())), preferred_element_type=F32)


def bits_of(n):
    return n.bit_length() - 1


def norm_forward(y_rows):
    centered = y_rows - jnp.mean(y_rows, axis=-1, keepdims=True)
    inverse = lax.rsqrt(jnp.mean(centered * centered, axis=-1, keepdims=True) + NORM_EPS)
    return centered * inverse, inverse


def norm_back(normed, inverse, upstream):
    mean_up = jnp.mean(upstream, axis=-1, keepdims=True)
    mean_cross = jnp.mean(upstream * normed, axis=-1, keepdims=True)
    return inverse * (upstream - mean_up - normed * mean_cross)


class Copies:
    def __init__(self, send, recv):
        self.send, self.recv, self.used = send, recv, 0

    def make(self, src, dst, device):
        n = self.used
        self.used += 1
        return pltpu.make_async_remote_copy(
            src_ref=src, dst_ref=dst, send_sem=self.send.at[n], recv_sem=self.recv.at[n],
            device_id=device, device_id_type=MESH,
        )


def kernel(nlat, nlon, t_hbm, c_hbm, wq_ref, wo_ref, gain_hbm, split_hbm, window_hbm, tau_ref,
           out_ref, gt_ref, g_ref,
           t_ref, c_ref, gain_ref, split_ref, window_ref, load, xs, xo, xq, w, tok, proj, qn, kn, probs, att, dy, da, dqkv, oq, oh,
           f0, f1, r0, r1, a0, a1, send, recv):
    lat, lon = lax.axis_index("lat"), lax.axis_index("lon")
    D = 512
    R = D // nlon
    H = R // 2
    H4 = R // 4
    xbit = (lat // 2) % 2
    core = lat % 2
    sibling = lat + 1 - 2 * core

    def flip(index, bit):
        v = (index // (1 << bit)) % 2
        return index + (1 - 2 * v) * (1 << bit), v

    def ahead(a, b):
        return ((lat + a) % nlat, (lon + b) % nlon)

    def behind(a, b):
        return ((lat + nlat - a) % nlat, (lon + nlon - b) % nlon)

    loads = [
        pltpu.make_async_copy(src, dst, load.at[n])
        for n, (src, dst) in enumerate((
            (t_hbm, t_ref), (c_hbm, c_ref), (split_hbm, split_ref),
            (window_hbm, window_ref), (gain_hbm, gain_ref),
            (wq_ref.at[:, pl.ds(0, D)], w.at[0, pl.ds(lon * R, R), :]),
            (wq_ref.at[:, pl.ds(D, D)], w.at[1, pl.ds(lon * R, R), :]),
            (wq_ref.at[:, pl.ds(2 * D, D)], w.at[2, pl.ds(lon * R, R), :]),
            (wo_ref, w.at[3, pl.ds(lon * R, R), :]),
        ))
    ]
    for c in loads:
        c.start()

    moves = ((0, 1), (1, 0), (1, 1))
    peers = [ahead(a, b) for a, b in moves] + [behind(a, b) for a, b in moves]
    core_group = [("lat", 0)]
    plane = [("lat", 1)] + [("lon", b) for b in reversed(range(bits_of(nlon)))]
    rest = [("lat", b) for b in range(2, bits_of(nlat))]
    strips = [("lat", 1)] + rest

    def member(group, k):
        at, place_mine, place_there = {"lat": lat, "lon": lon}, 0, 0
        for n, (axis, bit) in enumerate(group):
            there, mine = flip({"lat": lat, "lon": lon}[axis], bit)
            flipped = (k >> (len(group) - 1 - n)) & 1
            if flipped:
                at[axis] = at[axis] + (1 - 2 * mine) * (1 << bit)
            place_mine = 2 * place_mine + mine
            place_there = 2 * place_there + (1 - mine if flipped else mine)
        return (at["lat"], at["lon"]), place_mine, place_there

    for group in (core_group, plane, rest, strips):
        peers += [member(group, k)[0] for k in range(1, 1 << len(group))]
    barrier = pltpu.get_barrier_semaphore()
    for device in peers:
        pl.semaphore_signal(barrier, inc=1, device_id=device, device_id_type=MESH)
    pl.semaphore_wait(barrier, len(peers))

    copies = Copies(send, recv)
    waits = []

    mine4 = core * H + xbit * H4

    def w_source(p):
        if p < 3:
            return wq_ref.at[pl.ds(mine4, H4), pl.ds(p * D, D)]
        return wo_ref.at[pl.ds(mine4, H4), :]

    across, through, forward = [[], [], [], []], [], []

    def cross(p):
        for d in range(1, nlon):
            c = copies.make(w_source(p), w.at[p, pl.ds(lon * R + mine4, H4), :],
                            (lat, (lon + d) % nlon))
            c.start()
            across[p].append(c)

    for p in range(3):
        cross(p)

    xs[...] = jnp.zeros_like(xs)
    for c in loads[:3]:
        c.wait()
    halo = []
    for kind, ref in enumerate((t_ref, c_ref)):
        for r in range(WH):
            for col in range(WW):
                first = (r * WW + col) * 8
                xs[kind, first:first + LV, :] = ref[r, col].astype(F32)
        xo[kind] = dot(split_ref[...], xs[kind].astype(BF), 1, 0).astype(BF).reshape(4, 80, D)
        halo.append([])
        for a, b in moves:
            c = copies.make(xo.at[kind, 2 * a + b], xq.at[kind, 2 * (1 - a) + 1 - b], ahead(a, b))
            c.start()
            halo[kind].append(c)
        xq[kind, 3] = xo[kind, 0]
    cross(3)

    for p in range(4):
        one, two = [], []
        for d in range(1, nlon):
            there = ((lon + nlon - d) % nlon) * R
            part = w.at[p, pl.ds(there + mine4, H4), :]
            one.append(copies.make(part, part, (flip(lat, 1)[0], lon)))
            part = w.at[p, pl.ds(there + core * H, H), :]
            two.append(copies.make(part, part, (sibling, lon)))
        through.append(one)
        forward.append(two)

    for c in loads[3:]:
        c.wait()

    def windowed(kind):
        for c in halo[kind]:
            c.wait_recv()
        return dot(window_ref[...], xq[kind].reshape(320, D), 1, 0)

    def pass_on(before, after, p):
        for c in before[p]:
            c.wait_recv()
        for c in after[p]:
            c.start()

    def project(p):
        for c in forward[p]:
            c.wait_recv()
        proj[p] = dot(tok[...], w[p], 1, 0).astype(BF)

    for p in range(3):
        pass_on(across, through, p)
    tok[...] = windowed(0).astype(BF)
    for p in range(3):
        pass_on(through, forward, p)
        project(p)
    pass_on(across, through, 3)

    kk = lax.broadcasted_iota(jnp.int32, (144, 144), 0)
    qq = lax.broadcasted_iota(jnp.int32, (144, 144), 1)
    rows_ok = ((kk // 72) == (qq // 72)) | (jnp.zeros_like(kk) + lat != 0)
    level_ok = ((kk % 36) // 18) == ((qq % 36) // 18)

    def place(step):
        g, pair = step // 4, step % 4
        return (g, pair, pl.ds(pl.multiple_of(g * 144, 16), 144),
                pl.ds(pl.multiple_of(pair * 128, 128), 128))

    def halves(x):
        return x[:, :64], x[:, 64:]

    def unit(x):
        x = x.astype(F32)
        return (x * lax.rsqrt(jnp.sum(x * x, axis=-1, keepdims=True) + UNIT_EPS)).astype(BF)

    def twice(body):
        def run(n, carry):
            body(2 * n, carry)
            return body(2 * n + 1, carry)
        return run

    def forward_step(step, carry):
        g, pair, rs, cs = place(step)
        qs = [unit(x) for x in halves(proj[0, rs, cs])]
        ks = [unit(x) for x in halves(proj[1, rs, cs])]
        qn[rs, cs] = jnp.concatenate(qs, axis=1)
        kn[rs, cs] = jnp.concatenate(ks, axis=1)
        vs = halves(proj[2, rs, cs])
        mask = (rows_ok & (level_ok | (jnp.zeros_like(kk) + g == 1))).astype(F32)
        outs = []
        for i in range(2):
            s = dot(ks[i], qs[i], 1, 1) * tau_ref[2 * pair + i]
            e = jnp.exp(s) * mask
            p = e * (1.0 / jnp.sum(e, axis=0, keepdims=True))
            probs[2 * step + i] = p
            outs.append(dot(p.astype(BF), vs[i], 0, 0))
        att[rs, cs] = jnp.concatenate(outs, axis=1).astype(BF)
        return carry

    lax.fori_loop(0, 1, twice(forward_step), 0)
    pass_on(through, forward, 3)
    lax.fori_loop(1, 4, twice(forward_step), 0)
    cot = windowed(1)

    for c in forward[3]:
        c.wait_recv()
    normed, inverse = norm_forward(dot(att[...], w[3], 1, 0))
    gain = gain_ref[...]
    output = (tok[...].astype(F32) + gain * normed).astype(BF)
    homes = []

    def send_home(kind, value):
        oq[kind] = dot(window_ref[...], value, 0, 0).astype(BF).reshape(4, 80, D)
        for a, b in moves:
            c = copies.make(oq.at[kind, 2 * (1 - a) + 1 - b], oh.at[kind, 2 * a + b], behind(a, b))
            c.start()
            homes.append(c)
        oh[kind, 0] = oq[kind, 3]

    dy[...] = norm_back(normed, inverse, gain * cot).astype(BF)
    da[...] = dot(dy[...], w[3], 1, 1).astype(BF)

    def dv_step(step, carry):
        g, pair, rs, cs = place(step)
        das = halves(da[rs, cs])
        dqkv[2, rs, cs] = jnp.concatenate(
            [dot(probs[2 * step + i].astype(BF), das[i], 1, 0) for i in range(2)], axis=1
        ).astype(BF)
        return carry

    lax.fori_loop(0, 4, twice(dv_step), 0)

    half = 4 * D

    def place_gradient(f, which, grad):
        for b in range(nlon):
            for ch in range(4):
                first = which * half + (ch // 2) * (half // 2) + b * 2 * R + (ch % 2) * R
                f[first:first + R, :] = grad[b * R:(b + 1) * R, ch * 128:(ch + 1) * 128]

    class Stream:
        def __init__(self, f, r, a):
            self.f, self.r, self.a = f, r, a
            self.size, self.off, self.base = 2 * half, 0, 0
            self.gsize, self.goff = 2 * half // nlon, 0
            self.done = []

        def start(self, group):
            n = 1 << len(group)
            self.size //= n
            self.now = []
            for k in range(1, n):
                device, _, there = member(group, k)
                give = pl.multiple_of(self.off + there * self.size, 16)
                c = copies.make(self.f.at[pl.ds(give, self.size), :],
                                self.r.at[pl.ds(self.base, self.size), :], device)
                c.start()
                self.now.append((c, self.base))
                self.base += self.size
            self.off = self.off + member(group, 0)[1] * self.size
            for axis, bit in group:
                if axis == "lat":
                    self.gsize //= 2
                    self.goff = self.goff + flip(lat, bit)[1] * self.gsize

        def finish(self, last=False):
            keep = pl.ds(pl.multiple_of(self.off, 16), self.size)
            total = self.f[keep, :].astype(F32)
            for c, base in self.now:
                c.wait_recv()
                total = total + self.r[base:base + self.size, :].astype(F32)
            self.done += [c for c, _ in self.now]
            if last:
                self.a[pl.ds(pl.multiple_of(self.goff, 16), self.size), :] = total.astype(BF)
            else:
                self.f[keep, :] = total.astype(BF)

        def gather(self, group, off, size):
            self.now = []
            part = self.a.at[pl.ds(pl.multiple_of(off, 16), size), :]
            for k in range(1, 1 << len(group)):
                c = copies.make(part, part, member(group, k)[0])
                c.start()
                self.now.append((c, 0))

        def gathered(self):
            for c, _ in self.now:
                c.wait_recv()
                self.done.append(c)

    s0 = Stream(f0, r0, a0)
    s1 = Stream(f1, r1, a1)
    half_rows = half // nlon

    place_gradient(f0, 0, dot(att[...], dy[...], 0, 0).astype(BF))
    place_gradient(f0, 1, dot(tok[...], dqkv[2], 0, 0).astype(BF))
    s0.start(core_group)
    send_home(0, output)

    def back(x, n, grad):
        x = x.astype(F32)
        scale = lax.rsqrt(jnp.sum(x * x, axis=-1, keepdims=True) + UNIT_EPS)
        inner = jnp.sum(x * grad, axis=-1, keepdims=True)
        return scale * (grad - x * (inner * scale * scale))

    def ds_step(step, carry):
        g, pair, rs, cs = place(step)
        das, vs = halves(da[rs, cs]), halves(proj[2, rs, cs])
        qs, ks = halves(proj[0, rs, cs]), halves(proj[1, rs, cs])
        qns, kns = halves(qn[rs, cs]), halves(kn[rs, cs])
        dqs, dks = [], []
        for i in range(2):
            p = probs[2 * step + i]
            dp = dot(vs[i], das[i], 1, 1)
            tot = jnp.sum(p * dp, axis=0, keepdims=True)
            ds = (tau_ref[2 * pair + i] * (p * (dp - tot))).astype(BF)
            dqs.append(back(qs[i], qns[i], dot(ds, kns[i], 0, 0)))
            dks.append(back(ks[i], kns[i], dot(ds, qns[i], 1, 0)))
        dqkv[0, rs, cs] = jnp.concatenate(dqs, axis=1).astype(BF)
        dqkv[1, rs, cs] = jnp.concatenate(dks, axis=1).astype(BF)
        return carry

    lax.fori_loop(0, 1, twice(ds_step), 0)
    s0.finish()
    s0.start(plane)
    lax.fori_loop(1, 4, twice(ds_step), 0)
    place_gradient(f1, 0, dot(tok[...], dqkv[0], 0, 0).astype(BF))
    place_gradient(f1, 1, dot(tok[...], dqkv[1], 0, 0).astype(BF))
    s1.start(core_group)
    s0.finish()
    s0.start(rest)
    s1.finish()
    s1.start(plane)

    grad_in = dot(dqkv[0], w[0], 1, 1) + dot(dqkv[1], w[1], 1, 1) + dot(dqkv[2], w[2], 1, 1)
    send_home(1, (cot + grad_in).astype(BF))
    s0.finish(True)
    s0.gather(strips, s0.goff, s0.gsize)
    s1.finish()
    s1.start(rest)
    s0.gathered()
    s0.gather(core_group, core * half_rows, half_rows)
    s1.finish(True)
    s1.gather(strips, s1.goff, s1.gsize)

    def bring(kind, ref):
        for c in homes[3 * kind:3 * kind + 3]:
            c.wait_recv()
        full = dot(split_ref[...], oh[kind].reshape(320, D), 0, 0)
        for r in range(WH):
            for col in range(WW):
                first = (r * WW + col) * 8
                ref[r, col] = full[first:first + LV, :].astype(BF)

    def collect(a, p, which):
        for ch in range(4):
            first = which * half_rows + ch * R
            g_ref[:, p * D + ch * 128:p * D + (ch + 1) * 128] = a[first:first + R, :]

    bring(0, out_ref)
    bring(1, gt_ref)
    s0.gathered()
    collect(a0, 3, 0)
    collect(a0, 2, 1)
    s1.gathered()
    s1.gather(core_group, core * half_rows, half_rows)
    s1.gathered()
    collect(a1, 0, 0)
    collect(a1, 1, 1)
    started = sum(halo + across + through + forward, []) + homes
    for c in started + s0.done + s1.done:
        c.wait_send()


def on_device(nlat, nlon, tokens, w_qkv, w_out, gain, tau, cotangent):
    D = tokens.shape[3]

    split = np.zeros((320, 576), np.float32)
    window = np.zeros((288, 320), np.float32)
    for q in range(4):
        for i in range(72):
            level, row, col = LEVELS[i // 18], 3 * (q // 2) + i % 18 // 6, 6 * (q % 2) + i % 6
            split[q * 80 + i, (row * WW + col) * 8 + level] = 1
            window[i // 36 * 144 + q * 36 + i % 36, q * 80 + i] = 1
    R = D // nlon
    half = 4 * D
    n_copies = 12 + 12 * (nlon - 1) + 2 * (2 * nlon - 1 + nlat // 4 - 1 + nlat // 2 - 1 + 2)
    vm = pl.BlockSpec(memory_space=pltpu.VMEM)
    output, grad_tokens, grads = pl.pallas_call(
        functools.partial(kernel, nlat, nlon),
        out_shape=(
            jax.ShapeDtypeStruct((WH, WW, LV, D), BF),
            jax.ShapeDtypeStruct((WH, WW, LV, D), BF),
            jax.ShapeDtypeStruct((R, 4 * D), BF),
        ),
        in_specs=[pl.BlockSpec(memory_space=pl.ANY)] * 7 + [pl.BlockSpec(memory_space=pltpu.SMEM)],
        out_specs=(vm, vm, vm),
        scratch_shapes=[
            pltpu.VMEM((WH, WW, LV, D), BF),
            pltpu.VMEM((WH, WW, LV, D), BF),
            pltpu.VMEM((1, D), F32),
            pltpu.VMEM(split.shape, BF),
            pltpu.VMEM(window.shape, BF),
            pltpu.SemaphoreType.DMA((9,)),
            pltpu.VMEM((2, 576, D), F32),
            pltpu.VMEM((2, 4, 80, D), BF),
            pltpu.VMEM((2, 4, 80, D), BF),
            pltpu.VMEM((4, D, D), BF),
            pltpu.VMEM((288, D), BF),
            pltpu.VMEM((3, 288, D), BF),
            pltpu.VMEM((288, D), BF),
            pltpu.VMEM((288, D), BF),
            pltpu.VMEM((16, 144, 144), F32),
            pltpu.VMEM((288, D), BF),
            pltpu.VMEM((288, D), BF),
            pltpu.VMEM((288, D), BF),
            pltpu.VMEM((3, 288, D), BF),
            pltpu.VMEM((2, 4, 80, D), BF),
            pltpu.VMEM((2, 4, 80, D), BF),
            pltpu.VMEM((2 * half, 128), BF),
            pltpu.VMEM((2 * half, 128), BF),
            pltpu.VMEM((2 * half, 128), BF),
            pltpu.VMEM((2 * half, 128), BF),
            pltpu.VMEM((2 * half // nlon, 128), BF),
            pltpu.VMEM((2 * half // nlon, 128), BF),
            pltpu.SemaphoreType.DMA((n_copies,)),
            pltpu.SemaphoreType.DMA((n_copies,)),
        ],
        compiler_params=pltpu.CompilerParams(
            collective_id=0, has_side_effects=True, vmem_limit_bytes=60 * 1024 * 1024
        ),
    )(tokens.transpose(1, 2, 0, 3), cotangent.transpose(1, 2, 0, 3), w_qkv, w_out, gain.reshape(1, D), jnp.asarray(split, BF),
      jnp.asarray(window, BF), tau)

    return (
        output.transpose(2, 0, 1, 3),
        grad_tokens.transpose(2, 0, 1, 3),
        grads[:, : 3 * D].astype(F32),
        grads[:, 3 * D :].astype(F32),
    )


def solution(mesh):
    nlat, nlon = mesh.shape["lat"], mesh.shape["lon"]
    grid = P(None, "lat", "lon", None)
    rows = P("lon", None)
    return jax.shard_map(
        functools.partial(on_device, nlat, nlon),
        mesh=mesh,
        in_specs=(grid, rows, rows, P(), P(), grid),
        out_specs=(grid, grid, rows, rows),
        check_vma=False,
    )
```
